512 devices in a mesh: row: 16 (over z), col: 16 (over y_hi, x, core), chan: 2 (over y_lo).
Axes of the slice: x: 4, y: 4 (y_hi: 2, y_lo: 2; y = y_hi * 2 + y_lo), z: 16, core: 2. Of those that a mesh axis runs over, the one named last changes fastest.
Arguments:
- array_volts: bfloat16 [6, 2, 2048, 2048], P('chan', None, ('row', 'col')), parts along dimension 0, may hold values from -15 to 15, as said below
- reference_volts: bfloat16 [6, 2, 32, 2048], P('chan', None, None, 'col'), parts along dimension 0, may hold values from -15 to 15, as said below
Outputs:
- cleaned: float32 [6, 2, 2048, 2048], P('chan', None, 'row', 'col'), parts along dimension 0
The draws below stay inside these ranges and needn't reach their ends.
There are 2 independent parts, one for each index of `chan`. The reference program is written for one: setup_inputs(seed, part) draws one part's arguments, and reference() takes and returns one part's arrays. A program takes and returns all parts, laid end to end along the dimension named above; each array names one. Nothing has to cross between parts.
Inputs may be any that keep to these rules, and one draw needn't show every extreme that they name: `array_volts`: array voltages: common interference from a few sources plus independent noise. `reference_volts`: reference voltages: the same interference sources seen with other gains, plus independent noise.
All inputs are finite; a program needn't handle non-finite values.
Results may differ from the reference program's by a relative error of at most 0.0003.
Values may be sent and summed in bfloat16 or wider, within the bound.
A program may use at most 64 MiB of HBM per device.

```python
import jax
import jax.numpy as jnp
from jax import lax

DEVICE_ANTENNAS = 8
NREF = 32
SUBINT_SAMPLES = 2048
SUBS = 3
NA = 2048
N_ROW = 16
N_COL = 16


rfi_sources = 16


def common_signal(key):
    signal_key = jax.random.fold_in(key, 7001)
    return jax.random.normal(signal_key, (SUBS, 2, rfi_sources, SUBINT_SAMPLES), jnp.float32) * 0.7071


def apply_gains(gains, signal):
    real_part = jnp.einsum('nk,skt->snt', gains[0], signal[:, 0]) - jnp.einsum('nk,skt->snt', gains[1], signal[:, 1])
    imaginary_portion = jnp.einsum('nk,skt->snt', gains[0], signal[:, 1]) + jnp.einsum('nk,skt->snt', gains[1], signal[:, 0])
    return jnp.stack([real_part, imaginary_portion], 1)


def noise_field(key, count):
    scale_key = jax.random.fold_in(key, 1)
    value_key = jax.random.fold_in(key, 2)
    scales = jnp.exp(jax.random.uniform(scale_key, (count, 1), jnp.float32, jnp.log(0.5), jnp.log(1.5)))
    values = jax.random.normal(value_key, (SUBS, 2, count, SUBINT_SAMPLES), jnp.float32)
    return values * 0.7071 * scales


def draw_array_volts(key, part):
    signal = common_signal(key)
    gains = jax.random.normal(jax.random.fold_in(key, 7002), (2, NA, rfi_sources), jnp.float32) * jnp.sqrt(2.0 / rfi_sources)
    noise = noise_field(jax.random.fold_in(key, 7003), NA)
    return jnp.clip(apply_gains(gains, signal) + noise, -15.0, 15.0).astype(jnp.bfloat16)


def draw_reference_volts(key, part):
    signal = common_signal(key)
    gains = jax.random.normal(jax.random.fold_in(key, 7004), (2, NREF, rfi_sources), jnp.float32) * jnp.sqrt(0.05)
    noise = noise_field(jax.random.fold_in(key, 7005), NREF)
    return jnp.clip(apply_gains(gains, signal) + noise, -15.0, 15.0).astype(jnp.bfloat16)


def setup_inputs(seed: int = 0, part: int = 0) -> dict:
    key_list = jax.random.split(jax.random.key(seed), 3)
    part_keys = jax.random.split(jax.random.fold_in(key_list[2], part), 3)
    return {
        "array_volts": draw_array_volts(jax.random.fold_in(jax.random.fold_in(key_list[2], part), 71), part),
        "reference_volts": draw_reference_volts(jax.random.fold_in(jax.random.fold_in(key_list[2], part), 71), part),
    }


def correlate(first_rows, second_rows):
    width_first = first_rows.shape[1]
    width_second = second_rows.shape[1]
    samples = first_rows.shape[2]
    stacked_first = first_rows.reshape(2 * width_first, samples).astype(jnp.float32)
    stacked_second = second_rows.reshape(2 * width_second, samples).astype(jnp.float32)
    product = jnp.einsum('xn,yn->xy', stacked_first, stacked_second, precision=lax.Precision.HIGHEST)
    real_part = product[:width_first, :width_second] + product[width_first:, width_second:]
    imaginary_portion = product[width_first:, :width_second] - product[:width_first, width_second:]
    return jnp.stack([real_part, imaginary_portion]) / jnp.float32(samples)

def subtract(vis_tile, rows_cross, cross_cols, reference_covariance):
    real_cov = reference_covariance[0]
    imag_cov = reference_covariance[1]
    system = jnp.concatenate([jnp.concatenate([real_cov, -imag_cov], 1), jnp.concatenate([imag_cov, real_cov], 1)], 0)
    lower_factor = jnp.linalg.cholesky(system)
    right_hand = jnp.concatenate([cross_cols[0], cross_cols[1]], 0)
    middle = lax.linalg.triangular_solve(lower_factor, right_hand, left_side=True, lower=True)
    solved = lax.linalg.triangular_solve(lower_factor, middle, left_side=True, lower=True, transpose_a=True)
    half_size = real_cov.shape[0]
    solved_real = solved[:half_size]
    solved_imag = solved[half_size:]
    highest = lax.Precision.HIGHEST
    corr_real = jnp.dot(rows_cross[0], solved_real, precision=highest) - jnp.dot(rows_cross[1], solved_imag, precision=highest)
    corr_imag = jnp.dot(rows_cross[0], solved_imag, precision=highest) + jnp.dot(rows_cross[1], solved_real, precision=highest)
    return vis_tile - jnp.stack([corr_real, corr_imag])

def reference(array_volts, reference_volts):
    results = []
    for sub_index in range(SUBS):
        complete_matrix = array_volts[sub_index]
        antenna_list = complete_matrix.shape[1]
        permuted_rows = complete_matrix.reshape(2, N_ROW, N_COL, DEVICE_ANTENNAS, SUBINT_SAMPLES).transpose(0, 2, 1, 3, 4).reshape(2, antenna_list, SUBINT_SAMPLES)
        ref_all = reference_volts[sub_index]
        vis_tile = correlate(complete_matrix, permuted_rows)
        rows_cross = correlate(complete_matrix, ref_all)
        cross_cols = correlate(ref_all, permuted_rows)
        reference_covariance = correlate(ref_all, ref_all)
        results.append(subtract(vis_tile, rows_cross, cross_cols, reference_covariance))
    return jnp.stack(results)
```

```python
import functools

import jax
import jax.numpy as jnp
from jax import lax
from jax.experimental import pallas as pl
from jax.experimental.pallas import tpu as pltpu
from jax.sharding import PartitionSpec as P

MESH = pl.DeviceIdType.MESH
F32, BF16 = jnp.float32, jnp.bfloat16
SUBS, NREF, ANTS, SAMPLES = 3, 32, 8, 2048
ROWS, COLS, NX = 16, 16, 4
PAIR = 2 * ANTS
LANES = 512

FROM_Y, LEFT, RIGHT, LEFT_Y, RIGHT_Y, LEFT_2, RIGHT_2, OWN = range(8)


def kernel(volts, refs, out, colb, rowb, refb, ref_all, ref_mix, hi, lo, inv, *sems):
    z_send, z_recv, g_send, g_recv, c_send, c_recv = sems
    row, col = lax.axis_index("row"), lax.axis_index("col")
    up, down = lax.rem(row + 1, ROWS), lax.rem(row + ROWS - 1, ROWS)
    y, x, core = col // (2 * NX), lax.rem(col // 2, NX), lax.rem(col, 2)

    def at(dy, dx, other=False):
        yy = 1 - y if dy else y
        cc = 1 - core if other else core
        return yy * (2 * NX) + lax.rem(x + dx + NX, NX) * 2 + cc

    origin = {
        FROM_Y: at(1, 0), LEFT: at(0, -1), RIGHT: at(0, 1), LEFT_Y: at(1, -1),
        RIGHT_Y: at(1, 1), LEFT_2: at(0, 2), RIGHT_2: at(1, 2), OWN: col,
    }
    to_y, to_left, to_right, to_core = at(1, 0), at(0, -1), at(0, 1), at(0, 0, True)

    barrier = pltpu.get_barrier_semaphore()
    for axis, there in (
        ("row", up), ("row", down), ("col", to_y), ("col", to_left), ("col", to_right), ("col", to_core),
    ):
        pl.semaphore_signal(barrier, inc=1, device_id={axis: there}, device_id_type=MESH)
    pl.semaphore_wait(barrier, 6)

    def hops(way, sub):
        return 8 if (sub % 2) == way else 7

    def z_copy(way, hop, sub):
        start = lax.rem(row + (ROWS - hop if way == 0 else hop), ROWS)
        place = colb.at[sub, start]
        return pltpu.make_async_remote_copy(
            src_ref=volts.at[sub] if hop == 0 else place,
            dst_ref=place,
            send_sem=z_send.at[way, hop, sub],
            recv_sem=z_recv.at[way, hop, sub],
            device_id={"row": up if way == 0 else down},
            device_id_type=MESH,
        )

    def z_step(hop, sub):
        for way in range(2):
            if hop < hops(way, sub):
                z_copy(way, hop, sub).wait_recv()
                if hop + 1 < hops(way, sub):
                    z_copy(way, hop + 1, sub).start()

    def z_sent(hop):
        for way in range(2):
            for sub in range(SUBS):
                if hop < hops(way, sub):
                    z_copy(way, hop, sub).wait_send()

    def shard(kind, slot):
        return refb.at[slot] if kind == 0 else rowb.at[:, slot]

    def g_copy(kind, received, slot, there):
        mine = refs if kind == 0 else volts
        return pltpu.make_async_remote_copy(
            src_ref=mine if received in (FROM_Y, LEFT, RIGHT) else shard(kind, slot),
            dst_ref=shard(kind, slot),
            send_sem=g_send.at[kind, received],
            recv_sem=g_recv.at[kind, received],
            device_id={"col": there},
            device_id_type=MESH,
        )

    def g_send_copy(kind, received):
        slot, there = {
            FROM_Y: (col, to_y), LEFT: (col, to_right), RIGHT: (col, to_left),
            LEFT_Y: (origin[FROM_Y], to_right), RIGHT_Y: (origin[FROM_Y], to_left),
            LEFT_2: (origin[LEFT], to_right), RIGHT_2: (origin[RIGHT_Y], to_left),
        }[received]
        return g_copy(kind, received, slot, there)

    def core_copy(kind, received):
        slot = origin[received]
        mine = refs if kind == 0 else volts
        return pltpu.make_async_remote_copy(
            src_ref=mine if received == OWN else shard(kind, slot),
            dst_ref=shard(kind, slot),
            send_sem=c_send.at[kind, received],
            recv_sem=c_recv.at[kind, received],
            device_id={"col": to_core},
            device_id_type=MESH,
        )

    def g_start(kind):
        for received in (FROM_Y, LEFT, RIGHT):
            g_send_copy(kind, received).start()
        core_copy(kind, OWN).start()

    def g_arrived(kind, *those):
        for received in those:
            g_copy(kind, received, origin[received], to_left).wait_recv()
            core_copy(kind, received).start()

    def g_forward(kind, *those):
        for received in those:
            g_send_copy(kind, received).start()

    def core_arrived(kind):
        for received in range(8):
            core_copy(kind, received).wait_recv()

    def g_sent(kind):
        for received in range(7):
            g_send_copy(kind, received).wait_send()
        for received in range(8):
            core_copy(kind, received).wait_send()

    def gather_references():
        for sub in range(SUBS):
            whole = jnp.concatenate([refb[c, sub] for c in range(COLS)], axis=1)
            ref_all[sub] = whole
            real, imag = whole[:NREF], whole[NREF:]
            one = jnp.concatenate([real, -imag], axis=0)
            two = jnp.concatenate([imag, real], axis=0)
            ref_mix[sub, 0] = jnp.concatenate([one, one, one], axis=0)
            ref_mix[sub, 1] = jnp.concatenate([two, two, two], axis=0)

    def product(a, b):
        return lax.dot_general(a, b, (((1,), (1,)), ((), ())), preferred_element_type=F32)

    def covariance():
        for sub in range(SUBS):
            g = product(ref_all[sub], ref_all[sub])
            inv[0, sub] = g[:NREF, :NREF] + g[NREF:, NREF:]
            inv[1, sub] = g[NREF:, :NREF] - g[:NREF, NREF:]

    def eliminate(first, last):
        lane = lax.broadcasted_iota(jnp.int32, (SUBS, NREF, NREF), 2)
        line = lax.broadcasted_iota(jnp.int32, (SUBS, NREF, NREF), 1)

        def step(k, carry):
            re, im = carry
            on_lane, on_line = lane == k, line == k
            col_re = jnp.sum(jnp.where(on_lane, re, 0.0), axis=2, keepdims=True)
            col_im = jnp.sum(jnp.where(on_lane, im, 0.0), axis=2, keepdims=True)
            row_re = jnp.sum(jnp.where(on_line, re, 0.0), axis=1, keepdims=True)
            row_im = jnp.sum(jnp.where(on_line, im, 0.0), axis=1, keepdims=True)
            both = jnp.logical_and(on_lane, on_line)
            pivot = jnp.sum(
                jnp.sum(jnp.where(both, re, 0.0), axis=2, keepdims=True), axis=1, keepdims=True
            )
            scale = 1.0 / pivot
            first_lane = lax.broadcasted_iota(jnp.int32, (SUBS, 1, NREF), 2) == k
            row_re = jnp.where(first_lane, 1.0, row_re) * scale
            row_im = jnp.where(first_lane, 0.0, row_im) * scale
            new_re = jnp.where(on_lane, 0.0, re) - (col_re * row_re - col_im * row_im)
            new_im = jnp.where(on_lane, 0.0, im) - (col_re * row_im + col_im * row_re)
            return jnp.where(on_line, row_re, new_re), jnp.where(on_line, row_im, new_im)

        re, im = lax.fori_loop(first, last, step, (inv[0], inv[1]))
        inv[0] = re
        inv[1] = im

    def weights(sub):
        q = product(rowb[sub].reshape(COLS * PAIR, SAMPLES), ref_all[sub])
        q = q.reshape(COLS, 2, ANTS, 2 * NREF)
        cross_re = (q[:, 0, :, :NREF] + q[:, 1, :, NREF:]).reshape(COLS * ANTS, NREF)
        cross_im = (q[:, 1, :, :NREF] - q[:, 0, :, NREF:]).reshape(COLS * ANTS, NREF)
        re, im = inv[0, sub], inv[1, sub]
        cross = jnp.concatenate([cross_re, cross_im], axis=1)
        system = jnp.concatenate(
            [jnp.concatenate([re, im], axis=1), jnp.concatenate([-im, re], axis=1)], axis=0
        )
        w = jnp.dot(cross, system, precision=lax.Precision.HIGHEST, preferred_element_type=F32)
        w1 = w.astype(BF16)
        rest = w - w1.astype(F32)
        w2 = rest.astype(BF16)
        w3 = (rest - w2.astype(F32)).astype(BF16)
        return jnp.concatenate([w1, w2, w3], axis=1)

    def clean_rows(sub, w, part):
        here = pl.ds(part * LANES, LANES)
        raw = rowb[sub, :, :, here].astype(F32).reshape(COLS, 2, ANTS, LANES)
        for p in range(2):
            one = raw[:, p].reshape(COLS * ANTS, LANES)
            one = one - jnp.dot(w, ref_mix[sub, p, :, here], preferred_element_type=F32)
            top = one.astype(BF16)
            hi[sub, pl.ds(p * 128, 128), here] = top
            lo[sub, pl.ds(p * 128, 128), here] = (one - top.astype(F32)).astype(BF16)

    def finish(sub):
        b = colb[sub].reshape(ROWS * PAIR, SAMPLES)
        t = product(b, hi[sub]) + product(b, lo[sub])
        t = t.reshape(ROWS, 2, ANTS, 256)
        re = (t[:, 0, :, :128] + t[:, 1, :, 128:]).reshape(ROWS * ANTS, 128)
        im = (t[:, 0, :, 128:] - t[:, 1, :, :128]).reshape(ROWS * ANTS, 128)
        out[sub, 0] = re.T * (1.0 / SAMPLES)
        out[sub, 1] = im.T * (1.0 / SAMPLES)

    for sub in range(SUBS):
        for way in range(2):
            z_copy(way, 0, sub).start()
        if sub == 0:
            g_start(0)
    g_start(1)
    for sub in range(SUBS):
        colb[sub, row] = volts[sub]
        rowb[sub, col] = volts[sub]
    refb[col] = refs[...]

    z_step(0, 0)
    g_arrived(0, FROM_Y, LEFT, RIGHT)
    g_forward(0, LEFT_Y, RIGHT_Y, LEFT_2)
    z_step(0, 1)
    z_step(0, 2)
    g_arrived(0, LEFT_Y, RIGHT_Y, LEFT_2)
    g_forward(0, RIGHT_2)
    z_step(1, 0)
    g_arrived(1, FROM_Y, LEFT, RIGHT)
    g_forward(1, LEFT_Y, RIGHT_Y, LEFT_2)
    g_arrived(0, RIGHT_2)
    z_step(1, 1)
    z_step(1, 2)
    core_arrived(0)
    gather_references()
    z_step(2, 0)
    covariance()
    z_step(2, 1)
    eliminate(0, 6)
    z_step(2, 2)
    g_arrived(1, LEFT_Y, RIGHT_Y)
    g_forward(1, RIGHT_2)
    eliminate(6, 12)
    for sub in range(SUBS):
        z_step(3, sub)
        eliminate(12 + 6 * sub, 18 + 6 * sub)
    eliminate(30, 32)
    z_sent(0)
    z_step(4, 0)
    g_arrived(1, LEFT_2, RIGHT_2)
    z_step(4, 1)
    z_step(4, 2)
    z_sent(1)
    core_arrived(1)
    for sub in range(SUBS):
        w = weights(sub)
        z_step(5, sub)
        clean_rows(sub, w, 0)
        clean_rows(sub, w, 1)
        if sub > 0:
            z_step(6, sub - 1)
        clean_rows(sub, w, 2)
        clean_rows(sub, w, 3)
    g_sent(0)
    g_sent(1)
    z_step(6, 2)
    for hop in range(2, 6):
        z_sent(hop)
    for sub in range(SUBS):
        z_step(7, sub)
        finish(sub)
    z_sent(6)
    z_sent(7)


def per_device(array_volts, reference_volts):
    volts = array_volts.reshape(SUBS, PAIR, SAMPLES)
    refs = reference_volts.reshape(SUBS, 2 * NREF, SAMPLES // COLS)
    vmem = pl.BlockSpec(memory_space=pltpu.VMEM)
    return pl.pallas_call(
        kernel,
        out_shape=jax.ShapeDtypeStruct((SUBS, 2, COLS * ANTS, ROWS * ANTS), F32),
        in_specs=[vmem, vmem],
        out_specs=vmem,
        scratch_shapes=[
            pltpu.VMEM((SUBS, ROWS, PAIR, SAMPLES), BF16),
            pltpu.VMEM((SUBS, COLS, PAIR, SAMPLES), BF16),
            pltpu.VMEM((COLS, SUBS, 2 * NREF, SAMPLES // COLS), BF16),
            pltpu.VMEM((SUBS, 2 * NREF, SAMPLES), BF16),
            pltpu.VMEM((SUBS, 2, 6 * NREF, SAMPLES), BF16),
            pltpu.VMEM((SUBS, 2 * COLS * ANTS, SAMPLES), BF16),
            pltpu.VMEM((SUBS, 2 * COLS * ANTS, SAMPLES), BF16),
            pltpu.VMEM((2, SUBS, NREF, NREF), F32),
            pltpu.SemaphoreType.DMA((2, 8, SUBS)),
            pltpu.SemaphoreType.DMA((2, 8, SUBS)),
            pltpu.SemaphoreType.DMA((2, 7)),
            pltpu.SemaphoreType.DMA((2, 7)),
            pltpu.SemaphoreType.DMA((2, 8)),
            pltpu.SemaphoreType.DMA((2, 8)),
        ],
        compiler_params=pltpu.CompilerParams(
            collective_id=0, has_side_effects=True, vmem_limit_bytes=48 * 1024 * 1024
        ),
    )(volts, refs)


def solution(mesh):
    return jax.shard_map(
        per_device,
        mesh=mesh,
        in_specs=(P("chan", None, ("row", "col"), None), P("chan", None, None, "col")),
        out_specs=P("chan", None, "row", "col"),
        check_vma=False,
    )
```

```python
import functools

import jax
import jax.numpy as jnp
from jax import lax
from jax.experimental import pallas as pl
from jax.experimental.pallas import tpu as pltpu
from jax.sharding import PartitionSpec as P

MESH = pl.DeviceIdType.MESH
F32, BF16 = jnp.float32, jnp.bfloat16
SUBS, NREF, ANTS, SAMPLES = 3, 32, 8, 2048
ROWS, COLS, NX = 16, 16, 4
PAIR = 2 * ANTS
LANES = 512

FROM_Y, LEFT, RIGHT, LEFT_Y, RIGHT_Y, LEFT_2, RIGHT_2, OWN = range(8)


def kernel(volts, refs, out, colb, rowb, refb, ref_all, ref_mix, hi, lo, inv, *sems):
    z_send, z_recv, g_send, g_recv, c_send, c_recv = sems
    row, col = lax.axis_index("row"), lax.axis_index("col")
    up, down = lax.rem(row + 1, ROWS), lax.rem(row + ROWS - 1, ROWS)
    y, x, core = col // (2 * NX), lax.rem(col // 2, NX), lax.rem(col, 2)

    def at(dy, dx, other=False):
        yy = 1 - y if dy else y
        cc = 1 - core if other else core
        return yy * (2 * NX) + lax.rem(x + dx + NX, NX) * 2 + cc

    origin = {
        FROM_Y: at(1, 0), LEFT: at(0, -1), RIGHT: at(0, 1), LEFT_Y: at(1, -1),
        RIGHT_Y: at(1, 1), LEFT_2: at(0, 2), RIGHT_2: at(1, 2), OWN: col,
    }
    to_y, to_left, to_right, to_core = at(1, 0), at(0, -1), at(0, 1), at(0, 0, True)

    barrier = pltpu.get_barrier_semaphore()
    for axis, there in (
        ("row", up), ("row", down), ("col", to_y), ("col", to_left), ("col", to_right), ("col", to_core),
    ):
        pl.semaphore_signal(barrier, inc=1, device_id={axis: there}, device_id_type=MESH)
    pl.semaphore_wait(barrier, 6)

    def reach(way, start, sub):
        up_hops = 7 + jnp.asarray(sub != 1).astype(jnp.int32)
        return up_hops if way == 0 else ROWS - 1 - up_hops

    def z_start(way, hop, sub):
        return lax.rem(row + (ROWS - hop if way == 0 else hop), ROWS)

    def z_copy(way, hop, sub, mine=False):
        place = colb.at[sub, z_start(way, hop, sub)]
        return pltpu.make_async_remote_copy(
            src_ref=volts.at[sub] if mine else place,
            dst_ref=place,
            send_sem=z_send.at[way, hop, sub],
            recv_sem=z_recv.at[way, hop, sub],
            device_id={"row": up if way == 0 else down},
            device_id_type=MESH,
        )

    def z_event(way, n):
        hop, sub = n // SUBS, lax.rem(n, SUBS)
        hops = reach(way, z_start(way, hop + 1, sub), sub)

        @pl.when(hop + 1 <= hops)
        def _():
            z_copy(way, hop, sub).wait_recv()

        @pl.when(hop + 2 <= hops)
        def _():
            z_copy(way, hop + 1, sub).start()

    def z_step(n):
        z_event(0, n)
        z_event(1, n)

    def z_steps(first, last, job):
        def body(n, carry):
            z_step(n)
            job(n - first)
            return carry

        lax.fori_loop(first, last, body, jnp.int32(0))

    def z_sent(hop):
        for sub in range(SUBS):
            for way in range(2):
                if hop == 0:
                    z_copy(way, hop, sub, True).wait_send()
                else:
                    @pl.when(hop + 1 <= reach(way, z_start(way, hop, sub), sub))
                    def _():
                        z_copy(way, hop, sub).wait_send()

    def shard(kind, slot):
        return refb.at[slot] if kind == 0 else rowb.at[:, slot]

    def g_copy(kind, received, slot, there):
        mine = refs if kind == 0 else volts
        return pltpu.make_async_remote_copy(
            src_ref=mine if received in (FROM_Y, LEFT, RIGHT) else shard(kind, slot),
            dst_ref=shard(kind, slot),
            send_sem=g_send.at[kind, received],
            recv_sem=g_recv.at[kind, received],
            device_id={"col": there},
            device_id_type=MESH,
        )

    def g_send_copy(kind, received):
        slot, there = {
            FROM_Y: (col, to_y), LEFT: (col, to_right), RIGHT: (col, to_left),
            LEFT_Y: (origin[FROM_Y], to_right), RIGHT_Y: (origin[FROM_Y], to_left),
            LEFT_2: (origin[LEFT], to_right), RIGHT_2: (origin[RIGHT_Y], to_left),
        }[received]
        return g_copy(kind, received, slot, there)

    def core_copy(kind, received):
        slot = origin[received]
        mine = refs if kind == 0 else volts
        return pltpu.make_async_remote_copy(
            src_ref=mine if received == OWN else shard(kind, slot),
            dst_ref=shard(kind, slot),
            send_sem=c_send.at[kind, received],
            recv_sem=c_recv.at[kind, received],
            device_id={"col": to_core},
            device_id_type=MESH,
        )

    def g_start(kind):
        for received in (FROM_Y, LEFT, RIGHT):
            g_send_copy(kind, received).start()
        core_copy(kind, OWN).start()

    def g_arrived(kind, *those):
        for received in those:
            g_copy(kind, received, origin[received], to_left).wait_recv()
            core_copy(kind, received).start()

    def g_forward(kind, *those):
        for received in those:
            g_send_copy(kind, received).start()

    def core_arrived(kind):
        for received in range(8):
            core_copy(kind, received).wait_recv()

    def g_sent(kind):
        for received in range(7):
            g_send_copy(kind, received).wait_send()
        for received in range(8):
            core_copy(kind, received).wait_send()

    def gather_references():
        for sub in range(SUBS):
            whole = jnp.concatenate([refb[c, sub] for c in range(COLS)], axis=1)
            ref_all[sub] = whole
            real, imag = whole[:NREF], whole[NREF:]
            one = jnp.concatenate([real, -imag], axis=0)
            two = jnp.concatenate([imag, real], axis=0)
            ref_mix[sub, 0] = jnp.concatenate([one, one, one], axis=0)
            ref_mix[sub, 1] = jnp.concatenate([two, two, two], axis=0)

    def product(a, b):
        return lax.dot_general(a, b, (((1,), (1,)), ((), ())), preferred_element_type=F32)

    def covariance():
        for sub in range(SUBS):
            g = product(ref_all[sub], ref_all[sub])
            inv[0, sub] = g[:NREF, :NREF] + g[NREF:, NREF:]
            inv[1, sub] = g[NREF:, :NREF] - g[:NREF, NREF:]

    def eliminate(first, last):
        lane = lax.broadcasted_iota(jnp.int32, (SUBS, NREF, NREF), 2)
        line = lax.broadcasted_iota(jnp.int32, (SUBS, NREF, NREF), 1)

        def step(k, carry):
            re, im = carry
            on_lane, on_line = lane == k, line == k
            col_re = jnp.sum(jnp.where(on_lane, re, 0.0), axis=2, keepdims=True)
            col_im = jnp.sum(jnp.where(on_lane, im, 0.0), axis=2, keepdims=True)
            row_re = jnp.sum(jnp.where(on_line, re, 0.0), axis=1, keepdims=True)
            row_im = jnp.sum(jnp.where(on_line, im, 0.0), axis=1, keepdims=True)
            both = jnp.logical_and(on_lane, on_line)
            pivot = jnp.sum(
                jnp.sum(jnp.where(both, re, 0.0), axis=2, keepdims=True), axis=1, keepdims=True
            )
            scale = 1.0 / pivot
            first_lane = lax.broadcasted_iota(jnp.int32, (SUBS, 1, NREF), 2) == k
            row_re = jnp.where(first_lane, 1.0, row_re) * scale
            row_im = jnp.where(first_lane, 0.0, row_im) * scale
            new_re = jnp.where(on_lane, 0.0, re) - (col_re * row_re - col_im * row_im)
            new_im = jnp.where(on_lane, 0.0, im) - (col_re * row_im + col_im * row_re)
            return jnp.where(on_line, row_re, new_re), jnp.where(on_line, row_im, new_im)

        re, im = lax.fori_loop(first, last, step, (inv[0], inv[1]))
        inv[0] = re
        inv[1] = im

    def weights(sub):
        q = product(rowb[sub].reshape(COLS * PAIR, SAMPLES), ref_all[sub])
        q = q.reshape(COLS, 2, ANTS, 2 * NREF)
        cross_re = (q[:, 0, :, :NREF] + q[:, 1, :, NREF:]).reshape(COLS * ANTS, NREF)
        cross_im = (q[:, 1, :, :NREF] - q[:, 0, :, NREF:]).reshape(COLS * ANTS, NREF)
        re, im = inv[0, sub], inv[1, sub]
        cross = jnp.concatenate([cross_re, cross_im], axis=1)
        system = jnp.concatenate(
            [jnp.concatenate([re, im], axis=1), jnp.concatenate([-im, re], axis=1)], axis=0
        )
        w = jnp.dot(cross, system, precision=lax.Precision.HIGHEST, preferred_element_type=F32)
        w1 = w.astype(BF16)
        rest = w - w1.astype(F32)
        w2 = rest.astype(BF16)
        w3 = (rest - w2.astype(F32)).astype(BF16)
        return jnp.concatenate([w1, w2, w3], axis=1)

    def clean_rows(sub, w, part):
        here = pl.ds(part * LANES, LANES)
        raw = rowb[sub, :, :, here].astype(F32).reshape(COLS, 2, ANTS, LANES)
        for p in range(2):
            one = raw[:, p].reshape(COLS * ANTS, LANES)
            one = one - jnp.dot(w, ref_mix[sub, p, :, here], preferred_element_type=F32)
            top = one.astype(BF16)
            hi[sub, pl.ds(p * 128, 128), here] = top
            lo[sub, pl.ds(p * 128, 128), here] = (one - top.astype(F32)).astype(BF16)

    def finish(sub):
        b = colb[sub].reshape(ROWS * PAIR, SAMPLES)
        t = product(b, hi[sub]) + product(b, lo[sub])
        t = t.reshape(ROWS, 2, ANTS, 256)
        re = (t[:, 0, :, :128] + t[:, 1, :, 128:]).reshape(ROWS * ANTS, 128)
        im = (t[:, 0, :, 128:] - t[:, 1, :, :128]).reshape(ROWS * ANTS, 128)
        out[sub, 0] = re.T * (1.0 / SAMPLES)
        out[sub, 1] = im.T * (1.0 / SAMPLES)

    for sub in range(SUBS):
        for way in range(2):
            z_copy(way, 0, sub, True).start()
        if sub == 0:
            g_start(0)
    g_start(1)
    for sub in range(SUBS):
        colb[sub, row] = volts[sub]
        rowb[sub, col] = volts[sub]
    refb[col] = refs[...]

    def rows_first():
        g_arrived(1, FROM_Y, LEFT, RIGHT)
        g_forward(1, LEFT_Y, RIGHT_Y, LEFT_2)

    def rows_second():
        g_arrived(1, LEFT_Y, RIGHT_Y)
        g_forward(1, RIGHT_2)

    def refs_first():
        g_arrived(0, FROM_Y, LEFT, RIGHT)
        g_forward(0, LEFT_Y, RIGHT_Y, LEFT_2)

    def refs_second():
        g_arrived(0, LEFT_Y, RIGHT_Y, LEFT_2)
        g_forward(0, RIGHT_2)

    def refs_here():
        core_arrived(0)
        gather_references()

    def rows_done():
        g_arrived(1, LEFT_2, RIGHT_2)

    def eliminate_four(n):
        eliminate(4 * n, 4 * n + 4)

    def rows_cleaned(sub):
        w = weights(sub)
        for part in range(SAMPLES // LANES):
            clean_rows(sub, w, part)

    after = {
        1: refs_first, 3: refs_second, 4: rows_first, 5: functools.partial(g_arrived, 0, RIGHT_2),
        6: refs_here, 7: covariance,
    }
    for n in range(8):
        z_step(jnp.int32(n))
        if n in after:
            after[n]()
    z_steps(8, 12, eliminate_four)
    rows_second()
    z_steps(12, 16, lambda n: eliminate_four(n + 4))
    rows_done()
    z_step(jnp.int32(16))
    core_arrived(1)
    z_steps(17, 20, rows_cleaned)
    z_step(jnp.int32(20))
    for hop in range(6):
        z_sent(hop)
    g_sent(0)
    g_sent(1)
    z_steps(21, 24, finish)
    for hop in range(6, 8):
        z_sent(hop)


def per_device(array_volts, reference_volts):
    volts = array_volts.reshape(SUBS, PAIR, SAMPLES)
    refs = reference_volts.reshape(SUBS, 2 * NREF, SAMPLES // COLS)
    vmem = pl.BlockSpec(memory_space=pltpu.VMEM)
    return pl.pallas_call(
        kernel,
        out_shape=jax.ShapeDtypeStruct((SUBS, 2, COLS * ANTS, ROWS * ANTS), F32),
        in_specs=[vmem, vmem],
        out_specs=vmem,
        scratch_shapes=[
            pltpu.VMEM((SUBS, ROWS, PAIR, SAMPLES), BF16),
            pltpu.VMEM((SUBS, COLS, PAIR, SAMPLES), BF16),
            pltpu.VMEM((COLS, SUBS, 2 * NREF, SAMPLES // COLS), BF16),
            pltpu.VMEM((SUBS, 2 * NREF, SAMPLES), BF16),
            pltpu.VMEM((SUBS, 2, 6 * NREF, SAMPLES), BF16),
            pltpu.VMEM((SUBS, 2 * COLS * ANTS, SAMPLES), BF16),
            pltpu.VMEM((SUBS, 2 * COLS * ANTS, SAMPLES), BF16),
            pltpu.VMEM((2, SUBS, NREF, NREF), F32),
            pltpu.SemaphoreType.DMA((2, 8, SUBS)),
            pltpu.SemaphoreType.DMA((2, 8, SUBS)),
            pltpu.SemaphoreType.DMA((2, 7)),
            pltpu.SemaphoreType.DMA((2, 7)),
            pltpu.SemaphoreType.DMA((2, 8)),
            pltpu.SemaphoreType.DMA((2, 8)),
        ],
        compiler_params=pltpu.CompilerParams(
            collective_id=0, has_side_effects=True, vmem_limit_bytes=48 * 1024 * 1024
        ),
    )(volts, refs)


def solution(mesh):
    return jax.shard_map(
        per_device,
        mesh=mesh,
        in_specs=(P("chan", None, ("row", "col"), None), P("chan", None, None, "col")),
        out_specs=P("chan", None, "row", "col"),
        check_vma=False,
    )
```

```python
import functools

import jax
import jax.numpy as jnp
from jax import lax
from jax.experimental import pallas as pl
from jax.experimental.pallas import tpu as pltpu
from jax.sharding import PartitionSpec as P

MESH = pl.DeviceIdType.MESH
F32, BF16 = jnp.float32, jnp.bfloat16
SUBS, NREF, ANTS, SAMPLES = 3, 32, 8, 2048
ROWS, COLS, NX = 16, 16, 4
PAIR = 2 * ANTS
LANES = 512

FROM_Y, LEFT, RIGHT, LEFT_Y, RIGHT_Y, LEFT_2, RIGHT_2, OWN = range(8)


def kernel(volts, refs, out, colb, rowb, refb, ref_all, ref_mix, hi, lo, inv, *sems):
    z_send, z_recv, g_send, g_recv, c_send, c_recv, own_sem = sems
    row, col = lax.axis_index("row"), lax.axis_index("col")
    up, down = lax.rem(row + 1, ROWS), lax.rem(row + ROWS - 1, ROWS)
    y, x, core = col // (2 * NX), lax.rem(col // 2, NX), lax.rem(col, 2)

    def at(dy, dx, other=False):
        yy = 1 - y if dy else y
        cc = 1 - core if other else core
        return yy * (2 * NX) + lax.rem(x + dx + NX, NX) * 2 + cc

    origin = {
        FROM_Y: at(1, 0), LEFT: at(0, -1), RIGHT: at(0, 1), LEFT_Y: at(1, -1),
        RIGHT_Y: at(1, 1), LEFT_2: at(0, 2), RIGHT_2: at(1, 2), OWN: col,
    }
    to_y, to_left, to_right, to_core = at(1, 0), at(0, -1), at(0, 1), at(0, 0, True)

    barrier = pltpu.get_barrier_semaphore()
    for axis, there in (
        ("row", up), ("row", down), ("col", to_y), ("col", to_left), ("col", to_right), ("col", to_core),
    ):
        pl.semaphore_signal(barrier, inc=1, device_id={axis: there}, device_id_type=MESH)
    pl.semaphore_wait(barrier, 6)

    def reach(way, start, sub):
        up_hops = 7 + jnp.asarray(sub != 1).astype(jnp.int32)
        return up_hops if way == 0 else ROWS - 1 - up_hops

    def z_start(way, hop, sub):
        return lax.rem(row + (ROWS - hop if way == 0 else hop), ROWS)

    def z_copy(way, hop, sub, mine=False):
        place = colb.at[sub, z_start(way, hop, sub)]
        return pltpu.make_async_remote_copy(
            src_ref=volts.at[sub] if mine else place,
            dst_ref=place,
            send_sem=z_send.at[way, hop, sub],
            recv_sem=z_recv.at[way, hop, sub],
            device_id={"row": up if way == 0 else down},
            device_id_type=MESH,
        )

    def z_event(way, n):
        hop, sub = n // SUBS, lax.rem(n, SUBS)
        hops = reach(way, z_start(way, hop + 1, sub), sub)

        @pl.when(hop + 1 <= hops)
        def _():
            z_copy(way, hop, sub).wait_recv()

        @pl.when(hop + 2 <= hops)
        def _():
            z_copy(way, hop + 1, sub).start()

    def z_step(n):
        z_event(0, n)
        z_event(1, n)

    def z_steps(first, last, job):
        def body(n, carry):
            z_step(n)
            job(n - first)
            return carry

        lax.fori_loop(first, last, body, jnp.int32(0))

    def z_sent(hop):
        for sub in range(SUBS):
            for way in range(2):
                if hop == 0:
                    z_copy(way, hop, sub, True).wait_send()
                else:
                    @pl.when(hop + 1 <= reach(way, z_start(way, hop, sub), sub))
                    def _():
                        z_copy(way, hop, sub).wait_send()

    def shard(kind, slot):
        return refb.at[slot] if kind == 0 else rowb.at[:, slot]

    def g_copy(kind, received, slot, there):
        mine = refs if kind == 0 else volts
        return pltpu.make_async_remote_copy(
            src_ref=mine if received in (FROM_Y, LEFT, RIGHT) else shard(kind, slot),
            dst_ref=shard(kind, slot),
            send_sem=g_send.at[kind, received],
            recv_sem=g_recv.at[kind, received],
            device_id={"col": there},
            device_id_type=MESH,
        )

    def g_send_copy(kind, received):
        slot, there = {
            FROM_Y: (col, to_y), LEFT: (col, to_right), RIGHT: (col, to_left),
            LEFT_Y: (origin[FROM_Y], to_right), RIGHT_Y: (origin[FROM_Y], to_left),
            LEFT_2: (origin[LEFT], to_right), RIGHT_2: (origin[RIGHT_Y], to_left),
        }[received]
        return g_copy(kind, received, slot, there)

    def core_copy(kind, received):
        slot = origin[received]
        mine = refs if kind == 0 else volts
        return pltpu.make_async_remote_copy(
            src_ref=mine if received == OWN else shard(kind, slot),
            dst_ref=shard(kind, slot),
            send_sem=c_send.at[kind, received],
            recv_sem=c_recv.at[kind, received],
            device_id={"col": to_core},
            device_id_type=MESH,
        )

    def g_start(kind):
        for received in (FROM_Y, LEFT, RIGHT):
            g_send_copy(kind, received).start()
        core_copy(kind, OWN).start()

    def g_arrived(kind, *those):
        for received in those:
            g_copy(kind, received, origin[received], to_left).wait_recv()
            core_copy(kind, received).start()

    def g_forward(kind, *those):
        for received in those:
            g_send_copy(kind, received).start()

    def core_arrived(kind):
        for received in range(8):
            core_copy(kind, received).wait_recv()

    def g_sent(kind):
        for received in range(7):
            g_send_copy(kind, received).wait_send()
        for received in range(8):
            core_copy(kind, received).wait_send()

    def gather_references():
        for sub in range(SUBS):
            whole = jnp.concatenate([refb[c, sub] for c in range(COLS)], axis=1)
            ref_all[sub] = whole
            real, imag = whole[:NREF], whole[NREF:]
            one = jnp.concatenate([real, -imag], axis=0)
            two = jnp.concatenate([imag, real], axis=0)
            ref_mix[sub, 0] = jnp.concatenate([one, one, one], axis=0)
            ref_mix[sub, 1] = jnp.concatenate([two, two, two], axis=0)

    def product(a, b):
        return lax.dot_general(a, b, (((1,), (1,)), ((), ())), preferred_element_type=F32)

    def covariance():
        for sub in range(SUBS):
            g = product(ref_all[sub], ref_all[sub])
            inv[0, sub] = g[:NREF, :NREF] + g[NREF:, NREF:]
            inv[1, sub] = g[NREF:, :NREF] - g[:NREF, NREF:]

    def eliminate(first, last):
        lane = lax.broadcasted_iota(jnp.int32, (SUBS, NREF, NREF), 2)
        line = lax.broadcasted_iota(jnp.int32, (SUBS, NREF, NREF), 1)

        def step(k, carry):
            re, im = carry
            on_lane, on_line = lane == k, line == k
            col_re = jnp.sum(jnp.where(on_lane, re, 0.0), axis=2, keepdims=True)
            col_im = jnp.sum(jnp.where(on_lane, im, 0.0), axis=2, keepdims=True)
            row_re = jnp.sum(jnp.where(on_line, re, 0.0), axis=1, keepdims=True)
            row_im = jnp.sum(jnp.where(on_line, im, 0.0), axis=1, keepdims=True)
            both = jnp.logical_and(on_lane, on_line)
            pivot = jnp.sum(
                jnp.sum(jnp.where(both, re, 0.0), axis=2, keepdims=True), axis=1, keepdims=True
            )
            scale = 1.0 / pivot
            first_lane = lax.broadcasted_iota(jnp.int32, (SUBS, 1, NREF), 2) == k
            row_re = jnp.where(first_lane, 1.0, row_re) * scale
            row_im = jnp.where(first_lane, 0.0, row_im) * scale
            new_re = jnp.where(on_lane, 0.0, re) - (col_re * row_re - col_im * row_im)
            new_im = jnp.where(on_lane, 0.0, im) - (col_re * row_im + col_im * row_re)
            return jnp.where(on_line, row_re, new_re), jnp.where(on_line, row_im, new_im)

        re, im = lax.fori_loop(first, last, step, (inv[0], inv[1]))
        inv[0] = re
        inv[1] = im

    def weights(sub):
        q = product(rowb[sub].reshape(COLS * PAIR, SAMPLES), ref_all[sub])
        q = q.reshape(COLS, 2, ANTS, 2 * NREF)
        cross_re = (q[:, 0, :, :NREF] + q[:, 1, :, NREF:]).reshape(COLS * ANTS, NREF)
        cross_im = (q[:, 1, :, :NREF] - q[:, 0, :, NREF:]).reshape(COLS * ANTS, NREF)
        re, im = inv[0, sub], inv[1, sub]
        cross = jnp.concatenate([cross_re, cross_im], axis=1)
        system = jnp.concatenate(
            [jnp.concatenate([re, im], axis=1), jnp.concatenate([-im, re], axis=1)], axis=0
        )
        w = jnp.dot(cross, system, precision=lax.Precision.HIGHEST, preferred_element_type=F32)
        w1 = w.astype(BF16)
        rest = w - w1.astype(F32)
        w2 = rest.astype(BF16)
        w3 = (rest - w2.astype(F32)).astype(BF16)
        return jnp.concatenate([w1, w2, w3], axis=1)

    def clean_rows(sub, w, part):
        here = pl.ds(part * LANES, LANES)
        raw = rowb[sub, :, :, here].astype(F32).reshape(COLS, 2, ANTS, LANES)
        for p in range(2):
            one = raw[:, p].reshape(COLS * ANTS, LANES)
            one = one - jnp.dot(w, ref_mix[sub, p, :, here], preferred_element_type=F32)
            top = one.astype(BF16)
            hi[sub, pl.ds(p * 128, 128), here] = top
            lo[sub, pl.ds(p * 128, 128), here] = (one - top.astype(F32)).astype(BF16)

    def finish(sub):
        b = colb[sub].reshape(ROWS * PAIR, SAMPLES)
        t = product(b, hi[sub]) + product(b, lo[sub])
        t = t.reshape(ROWS, 2, ANTS, 256)
        re = (t[:, 0, :, :128] + t[:, 1, :, 128:]).reshape(ROWS * ANTS, 128)
        im = (t[:, 0, :, 128:] - t[:, 1, :, :128]).reshape(ROWS * ANTS, 128)
        out[sub, 0] = re.T * (1.0 / SAMPLES)
        out[sub, 1] = im.T * (1.0 / SAMPLES)

    for sub in range(SUBS):
        for way in range(2):
            z_copy(way, 0, sub, True).start()
        if sub == 0:
            g_start(0)
    g_start(1)
    own = [
        pltpu.make_async_copy(volts, colb.at[:, row], own_sem.at[0]),
        pltpu.make_async_copy(volts, rowb.at[:, col], own_sem.at[1]),
        pltpu.make_async_copy(refs, refb.at[col], own_sem.at[2]),
    ]
    for copy in own:
        copy.start()

    def rows_first():
        g_arrived(1, FROM_Y, LEFT, RIGHT)
        g_forward(1, LEFT_Y, RIGHT_Y, LEFT_2)

    def rows_second():
        g_arrived(1, LEFT_Y, RIGHT_Y)
        g_forward(1, RIGHT_2)

    def refs_first():
        g_arrived(0, FROM_Y, LEFT, RIGHT)
        g_forward(0, LEFT_Y, RIGHT_Y, LEFT_2)

    def refs_second():
        g_arrived(0, LEFT_Y, RIGHT_Y, LEFT_2)
        g_forward(0, RIGHT_2)

    def refs_here():
        core_arrived(0)
        gather_references()

    def rows_done():
        g_arrived(1, LEFT_2, RIGHT_2)

    def eliminate_four(n):
        eliminate(4 * n, 4 * n + 4)

    def rows_cleaned(sub):
        w = weights(sub)
        for part in range(SAMPLES // LANES):
            clean_rows(sub, w, part)

    after = {
        1: refs_first, 3: refs_second, 4: rows_first, 5: functools.partial(g_arrived, 0, RIGHT_2),
        6: refs_here, 7: covariance,
    }
    for n in range(8):
        z_step(jnp.int32(n))
        if n == 2:
            for copy in own:
                copy.wait()
        if n in after:
            after[n]()
    z_steps(8, 12, eliminate_four)
    rows_second()
    z_steps(12, 16, lambda n: eliminate_four(n + 4))
    rows_done()
    z_step(jnp.int32(16))
    core_arrived(1)
    z_steps(17, 20, rows_cleaned)
    z_step(jnp.int32(20))
    for hop in range(6):
        z_sent(hop)
    g_sent(0)
    g_sent(1)
    z_steps(21, 24, finish)
    for hop in range(6, 8):
        z_sent(hop)


def per_device(array_volts, reference_volts):
    volts = array_volts.reshape(SUBS, PAIR, SAMPLES)
    refs = reference_volts.reshape(SUBS, 2 * NREF, SAMPLES // COLS)
    vmem = pl.BlockSpec(memory_space=pltpu.VMEM)
    hbm = pl.BlockSpec(memory_space=pltpu.HBM)
    volts = pltpu.with_memory_space_constraint(volts, pltpu.HBM)
    refs = pltpu.with_memory_space_constraint(refs, pltpu.HBM)
    return pl.pallas_call(
        kernel,
        out_shape=jax.ShapeDtypeStruct((SUBS, 2, COLS * ANTS, ROWS * ANTS), F32),
        in_specs=[hbm, hbm],
        out_specs=vmem,
        scratch_shapes=[
            pltpu.VMEM((SUBS, ROWS, PAIR, SAMPLES), BF16),
            pltpu.VMEM((SUBS, COLS, PAIR, SAMPLES), BF16),
            pltpu.VMEM((COLS, SUBS, 2 * NREF, SAMPLES // COLS), BF16),
            pltpu.VMEM((SUBS, 2 * NREF, SAMPLES), BF16),
            pltpu.VMEM((SUBS, 2, 6 * NREF, SAMPLES), BF16),
            pltpu.VMEM((SUBS, 2 * COLS * ANTS, SAMPLES), BF16),
            pltpu.VMEM((SUBS, 2 * COLS * ANTS, SAMPLES), BF16),
            pltpu.VMEM((2, SUBS, NREF, NREF), F32),
            pltpu.SemaphoreType.DMA((2, 8, SUBS)),
            pltpu.SemaphoreType.DMA((2, 8, SUBS)),
            pltpu.SemaphoreType.DMA((2, 7)),
            pltpu.SemaphoreType.DMA((2, 7)),
            pltpu.SemaphoreType.DMA((2, 8)),
            pltpu.SemaphoreType.DMA((2, 8)),
            pltpu.SemaphoreType.DMA((3,)),
        ],
        compiler_params=pltpu.CompilerParams(
            collective_id=0, has_side_effects=True, vmem_limit_bytes=48 * 1024 * 1024
        ),
    )(volts, refs)


def solution(mesh):
    return jax.shard_map(
        per_device,
        mesh=mesh,
        in_specs=(P("chan", None, ("row", "col"), None), P("chan", None, None, "col")),
        out_specs=P("chan", None, "row", "col"),
        check_vma=False,
    )
```

```python
import functools

import jax
import jax.numpy as jnp
from jax import lax
from jax.experimental import pallas as pl
from jax.experimental.pallas import tpu as pltpu
from jax.sharding import PartitionSpec as P

MESH = pl.DeviceIdType.MESH
F32, BF16 = jnp.float32, jnp.bfloat16
SUBS, NREF, ANTS, SAMPLES = 3, 32, 8, 2048
ROWS, COLS, NX = 16, 16, 4
PAIR = 2 * ANTS
LANES = 512

FROM_Y, LEFT, RIGHT, LEFT_Y, RIGHT_Y, LEFT_2, RIGHT_2, OWN = range(8)


def kernel(volts, refs, out, colb, rowb, refb, ref_all, ref_mix, hi, lo, inv, *sems):
    z_send, z_recv, g_send, g_recv, c_send, c_recv, own_sem = sems
    row, col = lax.axis_index("row"), lax.axis_index("col")
    up, down = lax.rem(row + 1, ROWS), lax.rem(row + ROWS - 1, ROWS)
    y, x, core = col // (2 * NX), lax.rem(col // 2, NX), lax.rem(col, 2)

    def at(dy, dx, other=False):
        yy = 1 - y if dy else y
        cc = 1 - core if other else core
        return yy * (2 * NX) + lax.rem(x + dx + NX, NX) * 2 + cc

    origin = {
        FROM_Y: at(1, 0), LEFT: at(0, -1), RIGHT: at(0, 1), LEFT_Y: at(1, -1),
        RIGHT_Y: at(1, 1), LEFT_2: at(0, 2), RIGHT_2: at(1, 2), OWN: col,
    }
    to_y, to_left, to_right, to_core = at(1, 0), at(0, -1), at(0, 1), at(0, 0, True)

    barrier = pltpu.get_barrier_semaphore()
    for axis, there in (
        ("row", up), ("row", down), ("col", to_y), ("col", to_left), ("col", to_right), ("col", to_core),
    ):
        pl.semaphore_signal(barrier, inc=1, device_id={axis: there}, device_id_type=MESH)
    pl.semaphore_wait(barrier, 6)

    def reach(way, start, sub):
        up_hops = 7 + jnp.asarray(sub != 1).astype(jnp.int32)
        up_hops = jnp.where(start == 8, 7, up_hops)
        up_hops = jnp.where(start == 9, 7, up_hops)
        return up_hops if way == 0 else ROWS - 1 - up_hops

    def z_start(way, hop, sub):
        return lax.rem(row + (ROWS - hop if way == 0 else hop), ROWS)

    def z_copy(way, hop, sub, mine=False):
        place = colb.at[sub, z_start(way, hop, sub)]
        return pltpu.make_async_remote_copy(
            src_ref=volts.at[sub] if mine else place,
            dst_ref=place,
            send_sem=z_send.at[way, hop, sub],
            recv_sem=z_recv.at[way, hop, sub],
            device_id={"row": up if way == 0 else down},
            device_id_type=MESH,
        )

    def z_event(way, n):
        hop, sub = n // SUBS, lax.rem(n, SUBS)
        hops = reach(way, z_start(way, hop + 1, sub), sub)

        @pl.when(hop + 1 <= hops)
        def _():
            z_copy(way, hop, sub).wait_recv()

        @pl.when(hop + 2 <= hops)
        def _():
            z_copy(way, hop + 1, sub).start()

    def z_step(n):
        z_event(0, n)
        z_event(1, n)

    def z_steps(first, last, job):
        def body(n, carry):
            z_step(n)
            job(n - first)
            return carry

        lax.fori_loop(first, last, body, jnp.int32(0))

    def z_sent(hop):
        for sub in range(SUBS):
            for way in range(2):
                if hop == 0:
                    z_copy(way, hop, sub, True).wait_send()
                else:
                    @pl.when(hop + 1 <= reach(way, z_start(way, hop, sub), sub))
                    def _():
                        z_copy(way, hop, sub).wait_send()

    def shard(kind, slot):
        return refb.at[slot] if kind == 0 else rowb.at[:, slot]

    def g_copy(kind, received, slot, there):
        mine = refs if kind == 0 else volts
        return pltpu.make_async_remote_copy(
            src_ref=mine if received in (FROM_Y, LEFT, RIGHT) else shard(kind, slot),
            dst_ref=shard(kind, slot),
            send_sem=g_send.at[kind, received],
            recv_sem=g_recv.at[kind, received],
            device_id={"col": there},
            device_id_type=MESH,
        )

    def g_send_copy(kind, received):
        slot, there = {
            FROM_Y: (col, to_y), LEFT: (col, to_right), RIGHT: (col, to_left),
            LEFT_Y: (origin[FROM_Y], to_right), RIGHT_Y: (origin[FROM_Y], to_left),
            LEFT_2: (origin[LEFT], to_right), RIGHT_2: (origin[RIGHT_Y], to_left),
        }[received]
        return g_copy(kind, received, slot, there)

    def core_copy(kind, received):
        slot = origin[received]
        mine = refs if kind == 0 else volts
        return pltpu.make_async_remote_copy(
            src_ref=mine if received == OWN else shard(kind, slot),
            dst_ref=shard(kind, slot),
            send_sem=c_send.at[kind, received],
            recv_sem=c_recv.at[kind, received],
            device_id={"col": to_core},
            device_id_type=MESH,
        )

    def g_start(kind):
        for received in (FROM_Y, LEFT, RIGHT):
            g_send_copy(kind, received).start()
        core_copy(kind, OWN).start()

    def g_arrived(kind, *those):
        for received in those:
            g_copy(kind, received, origin[received], to_left).wait_recv()
            core_copy(kind, received).start()

    def g_forward(kind, *those):
        for received in those:
            g_send_copy(kind, received).start()

    def core_arrived(kind):
        for received in range(8):
            core_copy(kind, received).wait_recv()

    def g_sent(kind):
        for received in range(7):
            g_send_copy(kind, received).wait_send()
        for received in range(8):
            core_copy(kind, received).wait_send()

    def gather_references():
        for sub in range(SUBS):
            whole = jnp.concatenate([refb[c, sub] for c in range(COLS)], axis=1)
            ref_all[sub] = whole
            real, imag = whole[:NREF], whole[NREF:]
            one = jnp.concatenate([real, -imag], axis=0)
            two = jnp.concatenate([imag, real], axis=0)
            ref_mix[sub, 0] = jnp.concatenate([one, one, one], axis=0)
            ref_mix[sub, 1] = jnp.concatenate([two, two, two], axis=0)

    def product(a, b):
        return lax.dot_general(a, b, (((1,), (1,)), ((), ())), preferred_element_type=F32)

    def covariance():
        for sub in range(SUBS):
            g = product(ref_all[sub], ref_all[sub])
            inv[0, sub] = g[:NREF, :NREF] + g[NREF:, NREF:]
            inv[1, sub] = g[NREF:, :NREF] - g[:NREF, NREF:]

    def eliminate(first, last):
        lane = lax.broadcasted_iota(jnp.int32, (SUBS, NREF, NREF), 2)
        line = lax.broadcasted_iota(jnp.int32, (SUBS, NREF, NREF), 1)

        def step(k, carry):
            re, im = carry
            on_lane, on_line = lane == k, line == k
            col_re = jnp.sum(jnp.where(on_lane, re, 0.0), axis=2, keepdims=True)
            col_im = jnp.sum(jnp.where(on_lane, im, 0.0), axis=2, keepdims=True)
            row_re = jnp.sum(jnp.where(on_line, re, 0.0), axis=1, keepdims=True)
            row_im = jnp.sum(jnp.where(on_line, im, 0.0), axis=1, keepdims=True)
            first_lane = lax.broadcasted_iota(jnp.int32, (SUBS, 1, NREF), 2) == k
            pivot = jnp.sum(jnp.where(first_lane, row_re, 0.0), axis=2, keepdims=True)
            scale = 1.0 / pivot
            row_re = jnp.where(first_lane, 1.0, row_re) * scale
            row_im = jnp.where(first_lane, 0.0, row_im) * scale
            new_re = jnp.where(on_lane, 0.0, re) - (col_re * row_re - col_im * row_im)
            new_im = jnp.where(on_lane, 0.0, im) - (col_re * row_im + col_im * row_re)
            return jnp.where(on_line, row_re, new_re), jnp.where(on_line, row_im, new_im)

        re, im = lax.fori_loop(first, last, step, (inv[0], inv[1]))
        inv[0] = re
        inv[1] = im

    def weights(sub):
        q = product(rowb[sub].reshape(COLS * PAIR, SAMPLES), ref_all[sub])
        q = q.reshape(COLS, 2, ANTS, 2 * NREF)
        cross_re = (q[:, 0, :, :NREF] + q[:, 1, :, NREF:]).reshape(COLS * ANTS, NREF)
        cross_im = (q[:, 1, :, :NREF] - q[:, 0, :, NREF:]).reshape(COLS * ANTS, NREF)
        re, im = inv[0, sub], inv[1, sub]
        cross = jnp.concatenate([cross_re, cross_im], axis=1)
        system = jnp.concatenate(
            [jnp.concatenate([re, im], axis=1), jnp.concatenate([-im, re], axis=1)], axis=0
        )
        w = jnp.dot(cross, system, precision=lax.Precision.HIGHEST, preferred_element_type=F32)
        w1 = w.astype(BF16)
        rest = w - w1.astype(F32)
        w2 = rest.astype(BF16)
        w3 = (rest - w2.astype(F32)).astype(BF16)
        return jnp.concatenate([w1, w2, w3], axis=1)

    def clean_rows(sub, w, part):
        here = pl.ds(part * LANES, LANES)
        raw = rowb[sub, :, :, here].astype(F32).reshape(COLS, 2, ANTS, LANES)
        for p in range(2):
            one = raw[:, p].reshape(COLS * ANTS, LANES)
            one = one - jnp.dot(w, ref_mix[sub, p, :, here], preferred_element_type=F32)
            top = one.astype(BF16)
            hi[sub, pl.ds(p * 128, 128), here] = top
            lo[sub, pl.ds(p * 128, 128), here] = (one - top.astype(F32)).astype(BF16)

    def finish(sub):
        b = colb[sub].reshape(ROWS * PAIR, SAMPLES)
        t = product(b, hi[sub]) + product(b, lo[sub])
        t = t.reshape(ROWS, 2, ANTS, 256)
        re = (t[:, 0, :, :128] + t[:, 1, :, 128:]).reshape(ROWS * ANTS, 128)
        im = (t[:, 0, :, 128:] - t[:, 1, :, :128]).reshape(ROWS * ANTS, 128)
        out[sub, 0] = re.T * (1.0 / SAMPLES)
        out[sub, 1] = im.T * (1.0 / SAMPLES)

    for sub in range(SUBS):
        for way in range(2):
            z_copy(way, 0, sub, True).start()
        if sub == 0:
            g_start(0)
    g_start(1)
    own = [
        pltpu.make_async_copy(volts, colb.at[:, row], own_sem.at[0]),
        pltpu.make_async_copy(volts, rowb.at[:, col], own_sem.at[1]),
        pltpu.make_async_copy(refs, refb.at[col], own_sem.at[2]),
    ]
    for copy in own:
        copy.start()

    def rows_first():
        g_arrived(1, FROM_Y, LEFT, RIGHT)
        g_forward(1, LEFT_Y, RIGHT_Y, LEFT_2)

    def rows_second():
        g_arrived(1, LEFT_Y, RIGHT_Y)
        g_forward(1, RIGHT_2)

    def refs_first():
        g_arrived(0, FROM_Y, LEFT, RIGHT)
        g_forward(0, LEFT_Y, RIGHT_Y, LEFT_2)

    def refs_second():
        g_arrived(0, LEFT_Y, RIGHT_Y, LEFT_2)
        g_forward(0, RIGHT_2)

    def refs_here():
        core_arrived(0)
        gather_references()

    def eliminate_some(n):
        eliminate(5 * n, jnp.minimum(5 * n + 5, NREF))

    def rows_cleaned(sub):
        w = weights(sub)
        for part in range(SAMPLES // LANES):
            clean_rows(sub, w, part)

    after = {
        1: [refs_first], 3: [refs_second], 4: [rows_first], 5: [functools.partial(g_arrived, 0, RIGHT_2)],
        6: [refs_here], 7: [covariance],
    }
    for n in range(8):
        z_step(jnp.int32(n))
        if n == 2:
            for copy in own:
                copy.wait()
        for job in after.get(n, ()):
            job()
    z_steps(8, 9, eliminate_some)
    g_arrived(1, RIGHT_Y)
    g_forward(1, RIGHT_2)
    z_steps(9, 12, lambda n: eliminate_some(n + 1))
    g_arrived(1, LEFT_Y, LEFT_2)
    z_steps(12, 14, lambda n: eliminate_some(n + 4))
    g_arrived(1, RIGHT_2)
    z_steps(14, 15, lambda n: eliminate_some(n + 6))
    core_arrived(1)
    z_steps(15, 18, rows_cleaned)
    z_step(jnp.int32(18))
    z_step(jnp.int32(19))
    z_step(jnp.int32(20))
    for hop in range(6):
        z_sent(hop)
    g_sent(0)
    g_sent(1)
    z_steps(21, 24, finish)
    for hop in range(6, 8):
        z_sent(hop)


def per_device(array_volts, reference_volts):
    volts = array_volts.reshape(SUBS, PAIR, SAMPLES)
    refs = reference_volts.reshape(SUBS, 2 * NREF, SAMPLES // COLS)
    vmem = pl.BlockSpec(memory_space=pltpu.VMEM)
    hbm = pl.BlockSpec(memory_space=pltpu.HBM)
    volts = pltpu.with_memory_space_constraint(volts, pltpu.HBM)
    refs = pltpu.with_memory_space_constraint(refs, pltpu.HBM)
    return pl.pallas_call(
        kernel,
        out_shape=jax.ShapeDtypeStruct((SUBS, 2, COLS * ANTS, ROWS * ANTS), F32),
        in_specs=[hbm, hbm],
        out_specs=vmem,
        scratch_shapes=[
            pltpu.VMEM((SUBS, ROWS, PAIR, SAMPLES), BF16),
            pltpu.VMEM((SUBS, COLS, PAIR, SAMPLES), BF16),
            pltpu.VMEM((COLS, SUBS, 2 * NREF, SAMPLES // COLS), BF16),
            pltpu.VMEM((SUBS, 2 * NREF, SAMPLES), BF16),
            pltpu.VMEM((SUBS, 2, 6 * NREF, SAMPLES), BF16),
            pltpu.VMEM((SUBS, 2 * COLS * ANTS, SAMPLES), BF16),
            pltpu.VMEM((SUBS, 2 * COLS * ANTS, SAMPLES), BF16),
            pltpu.VMEM((2, SUBS, NREF, NREF), F32),
            pltpu.SemaphoreType.DMA((2, 9, SUBS)),
            pltpu.SemaphoreType.DMA((2, 9, SUBS)),
            pltpu.SemaphoreType.DMA((2, 7)),
            pltpu.SemaphoreType.DMA((2, 7)),
            pltpu.SemaphoreType.DMA((2, 8)),
            pltpu.SemaphoreType.DMA((2, 8)),
            pltpu.SemaphoreType.DMA((3,)),
        ],
        compiler_params=pltpu.CompilerParams(
            collective_id=0, has_side_effects=True, vmem_limit_bytes=48 * 1024 * 1024
        ),
    )(volts, refs)


def solution(mesh):
    return jax.shard_map(
        per_device,
        mesh=mesh,
        in_specs=(P("chan", None, ("row", "col"), None), P("chan", None, None, "col")),
        out_specs=P("chan", None, "row", "col"),
        check_vma=False,
    )
```

```python
import functools

import jax
import jax.numpy as jnp
from jax import lax
from jax.experimental import pallas as pl
from jax.experimental.pallas import tpu as pltpu
from jax.sharding import PartitionSpec as P

MESH = pl.DeviceIdType.MESH
F32, BF16 = jnp.float32, jnp.bfloat16
SUBS, NREF, ANTS, SAMPLES = 3, 32, 8, 2048
ROWS, COLS, NX = 16, 16, 4
PAIR = 2 * ANTS
LANES = 512

FROM_Y, LEFT, RIGHT, LEFT_Y, RIGHT_Y, LEFT_2, RIGHT_2, OWN = range(8)


def kernel(volts, refs, out, colb, rowb, refb, ref_all, ref_mix, hi, lo, inv, *sems):
    z_send, z_recv, g_send, g_recv, c_send, c_recv, own_sem = sems
    row, col = lax.axis_index("row"), lax.axis_index("col")
    up, down = lax.rem(row + 1, ROWS), lax.rem(row + ROWS - 1, ROWS)
    y, x, core = col // (2 * NX), lax.rem(col // 2, NX), lax.rem(col, 2)

    def at(dy, dx, other=False):
        yy = 1 - y if dy else y
        cc = 1 - core if other else core
        return yy * (2 * NX) + lax.rem(x + dx + NX, NX) * 2 + cc

    origin = {
        FROM_Y: at(1, 0), LEFT: at(0, -1), RIGHT: at(0, 1), LEFT_Y: at(1, -1),
        RIGHT_Y: at(1, 1), LEFT_2: at(0, 2), RIGHT_2: at(1, 2), OWN: col,
    }
    to_y, to_left, to_right, to_core = at(1, 0), at(0, -1), at(0, 1), at(0, 0, True)

    barrier = pltpu.get_barrier_semaphore()
    for axis, there in (
        ("row", up), ("row", down), ("col", to_y), ("col", to_left), ("col", to_right), ("col", to_core),
    ):
        pl.semaphore_signal(barrier, inc=1, device_id={axis: there}, device_id_type=MESH)
    pl.semaphore_wait(barrier, 6)

    def reach(way, start, sub):
        up_hops = 7 + jnp.asarray(sub != 1).astype(jnp.int32)
        up_hops = jnp.where(start == 8, 7, up_hops)
        up_hops = jnp.where(start == 9, 7, up_hops)
        up_hops = jnp.where(start == 10, 7, up_hops)
        up_hops = jnp.where(start == 11, 7, up_hops)
        return up_hops if way == 0 else ROWS - 1 - up_hops

    def z_start(way, hop, sub):
        return lax.rem(row + (ROWS - hop if way == 0 else hop), ROWS)

    def z_copy(way, hop, sub, mine=False):
        place = colb.at[sub, z_start(way, hop, sub)]
        return pltpu.make_async_remote_copy(
            src_ref=volts.at[sub] if mine else place,
            dst_ref=place,
            send_sem=z_send.at[way, hop, sub],
            recv_sem=z_recv.at[way, hop, sub],
            device_id={"row": up if way == 0 else down},
            device_id_type=MESH,
        )

    def z_event(way, n):
        hop, sub = n // SUBS, lax.rem(n, SUBS)
        hops = reach(way, z_start(way, hop + 1, sub), sub)

        @pl.when(hop + 1 <= hops)
        def _():
            z_copy(way, hop, sub).wait_recv()

        @pl.when(hop + 2 <= hops)
        def _():
            z_copy(way, hop + 1, sub).start()

    def z_step(n):
        z_event(0, n)
        z_event(1, n)

    def z_steps(first, last, job):
        def body(n, carry):
            z_step(n)
            job(n - first)
            return carry

        lax.fori_loop(first, last, body, jnp.int32(0))

    def z_sent(hop):
        for sub in range(SUBS):
            for way in range(2):
                if hop == 0:
                    z_copy(way, hop, sub, True).wait_send()
                else:
                    @pl.when(hop + 1 <= reach(way, z_start(way, hop, sub), sub))
                    def _():
                        z_copy(way, hop, sub).wait_send()

    def shard(kind, slot):
        return refb.at[slot] if kind == 0 else rowb.at[:, slot]

    def g_copy(kind, received, slot, there):
        mine = refs if kind == 0 else volts
        return pltpu.make_async_remote_copy(
            src_ref=mine if received in (FROM_Y, LEFT, RIGHT) else shard(kind, slot),
            dst_ref=shard(kind, slot),
            send_sem=g_send.at[kind, received],
            recv_sem=g_recv.at[kind, received],
            device_id={"col": there},
            device_id_type=MESH,
        )

    def g_send_copy(kind, received):
        slot, there = {
            FROM_Y: (col, to_y), LEFT: (col, to_right), RIGHT: (col, to_left),
            LEFT_Y: (origin[FROM_Y], to_right), RIGHT_Y: (origin[FROM_Y], to_left),
            LEFT_2: (origin[LEFT], to_right), RIGHT_2: (origin[RIGHT_Y], to_left),
        }[received]
        return g_copy(kind, received, slot, there)

    def core_copy(kind, received):
        slot = origin[received]
        mine = refs if kind == 0 else volts
        return pltpu.make_async_remote_copy(
            src_ref=mine if received == OWN else shard(kind, slot),
            dst_ref=shard(kind, slot),
            send_sem=c_send.at[kind, received],
            recv_sem=c_recv.at[kind, received],
            device_id={"col": to_core},
            device_id_type=MESH,
        )

    def g_start(kind):
        for received in (FROM_Y, LEFT, RIGHT):
            g_send_copy(kind, received).start()
        core_copy(kind, OWN).start()

    def g_arrived(kind, *those):
        for received in those:
            g_copy(kind, received, origin[received], to_left).wait_recv()
            core_copy(kind, received).start()

    def g_forward(kind, *those):
        for received in those:
            g_send_copy(kind, received).start()

    def core_arrived(kind):
        for received in range(8):
            core_copy(kind, received).wait_recv()

    def g_sent(kind):
        for received in range(7):
            g_send_copy(kind, received).wait_send()
        for received in range(8):
            core_copy(kind, received).wait_send()

    def gather_references():
        for sub in range(SUBS):
            whole = jnp.concatenate([refb[c, sub] for c in range(COLS)], axis=1)
            ref_all[sub] = whole
            real, imag = whole[:NREF], whole[NREF:]
            one = jnp.concatenate([real, -imag], axis=0)
            two = jnp.concatenate([imag, real], axis=0)
            ref_mix[sub, 0] = jnp.concatenate([one, one, one], axis=0)
            ref_mix[sub, 1] = jnp.concatenate([two, two, two], axis=0)

    def product(a, b):
        return lax.dot_general(a, b, (((1,), (1,)), ((), ())), preferred_element_type=F32)

    def covariance():
        for sub in range(SUBS):
            g = product(ref_all[sub], ref_all[sub])
            inv[0, sub] = g[:NREF, :NREF] + g[NREF:, NREF:]
            inv[1, sub] = g[NREF:, :NREF] - g[:NREF, NREF:]

    def eliminate(first, last):
        lane = lax.broadcasted_iota(jnp.int32, (SUBS, NREF, NREF), 2)
        line = lax.broadcasted_iota(jnp.int32, (SUBS, NREF, NREF), 1)

        def step(k, carry):
            re, im = carry
            on_lane, on_line = lane == k, line == k
            col_re = jnp.sum(jnp.where(on_lane, re, 0.0), axis=2, keepdims=True)
            col_im = jnp.sum(jnp.where(on_lane, im, 0.0), axis=2, keepdims=True)
            row_re = jnp.sum(jnp.where(on_line, re, 0.0), axis=1, keepdims=True)
            row_im = jnp.sum(jnp.where(on_line, im, 0.0), axis=1, keepdims=True)
            first_lane = lax.broadcasted_iota(jnp.int32, (SUBS, 1, NREF), 2) == k
            pivot = jnp.sum(jnp.where(first_lane, row_re, 0.0), axis=2, keepdims=True)
            scale = 1.0 / pivot
            row_re = jnp.where(first_lane, 1.0, row_re) * scale
            row_im = jnp.where(first_lane, 0.0, row_im) * scale
            new_re = jnp.where(on_lane, 0.0, re) - (col_re * row_re - col_im * row_im)
            new_im = jnp.where(on_lane, 0.0, im) - (col_re * row_im + col_im * row_re)
            return jnp.where(on_line, row_re, new_re), jnp.where(on_line, row_im, new_im)

        re, im = lax.fori_loop(first, last, step, (inv[0], inv[1]))
        inv[0] = re
        inv[1] = im

    def weights(sub):
        q = product(rowb[sub].reshape(COLS * PAIR, SAMPLES), ref_all[sub])
        q = q.reshape(COLS, 2, ANTS, 2 * NREF)
        cross_re = (q[:, 0, :, :NREF] + q[:, 1, :, NREF:]).reshape(COLS * ANTS, NREF)
        cross_im = (q[:, 1, :, :NREF] - q[:, 0, :, NREF:]).reshape(COLS * ANTS, NREF)
        re, im = inv[0, sub], inv[1, sub]
        cross = jnp.concatenate([cross_re, cross_im], axis=1)
        system = jnp.concatenate(
            [jnp.concatenate([re, im], axis=1), jnp.concatenate([-im, re], axis=1)], axis=0
        )
        w = jnp.dot(cross, system, precision=lax.Precision.HIGHEST, preferred_element_type=F32)
        w1 = w.astype(BF16)
        rest = w - w1.astype(F32)
        w2 = rest.astype(BF16)
        w3 = (rest - w2.astype(F32)).astype(BF16)
        return jnp.concatenate([w1, w2, w3], axis=1)

    def clean_rows(sub, w, part):
        here = pl.ds(part * LANES, LANES)
        raw = rowb[sub, :, :, here].astype(F32).reshape(COLS, 2, ANTS, LANES)
        for p in range(2):
            one = raw[:, p].reshape(COLS * ANTS, LANES)
            one = one - jnp.dot(w, ref_mix[sub, p, :, here], preferred_element_type=F32)
            top = one.astype(BF16)
            hi[sub, pl.ds(p * 128, 128), here] = top
            lo[sub, pl.ds(p * 128, 128), here] = (one - top.astype(F32)).astype(BF16)

    def finish(sub):
        b = colb[sub].reshape(ROWS * PAIR, SAMPLES)
        t = product(b, hi[sub]) + product(b, lo[sub])
        t = t.reshape(ROWS, 2, ANTS, 256)
        re = (t[:, 0, :, :128] + t[:, 1, :, 128:]).reshape(ROWS * ANTS, 128)
        im = (t[:, 0, :, 128:] - t[:, 1, :, :128]).reshape(ROWS * ANTS, 128)
        out[sub, 0] = re.T * (1.0 / SAMPLES)
        out[sub, 1] = im.T * (1.0 / SAMPLES)

    for sub in range(SUBS):
        for way in range(2):
            z_copy(way, 0, sub, True).start()
        if sub == 0:
            g_start(0)
    g_start(1)
    own = [
        pltpu.make_async_copy(volts, colb.at[:, row], own_sem.at[0]),
        pltpu.make_async_copy(volts, rowb.at[:, col], own_sem.at[1]),
        pltpu.make_async_copy(refs, refb.at[col], own_sem.at[2]),
    ]
    for copy in own:
        copy.start()

    def rows_first():
        g_arrived(1, FROM_Y, LEFT, RIGHT)
        g_forward(1, LEFT_Y, RIGHT_Y, LEFT_2)

    def rows_second():
        g_arrived(1, LEFT_Y, RIGHT_Y)
        g_forward(1, RIGHT_2)

    def refs_first():
        g_arrived(0, FROM_Y, LEFT, RIGHT)
        g_forward(0, LEFT_Y, RIGHT_Y, LEFT_2)

    def refs_second():
        g_arrived(0, LEFT_Y, RIGHT_Y, LEFT_2)
        g_forward(0, RIGHT_2)

    def refs_here():
        core_arrived(0)
        gather_references()

    def eliminate_some(n):
        eliminate(5 * n, jnp.minimum(5 * n + 5, NREF))

    def rows_cleaned(sub):
        w = weights(sub)
        for part in range(SAMPLES // LANES):
            clean_rows(sub, w, part)

    after = {
        1: [refs_first], 3: [refs_second], 4: [rows_first], 5: [functools.partial(g_arrived, 0, RIGHT_2)],
        6: [refs_here], 7: [covariance],
    }
    for n in range(8):
        z_step(jnp.int32(n))
        if n == 2:
            for copy in own:
                copy.wait()
        for job in after.get(n, ()):
            job()
    z_steps(8, 9, eliminate_some)
    g_arrived(1, RIGHT_Y)
    g_forward(1, RIGHT_2)
    z_steps(9, 12, lambda n: eliminate_some(n + 1))
    g_arrived(1, LEFT_Y, LEFT_2)
    z_steps(12, 14, lambda n: eliminate_some(n + 4))
    g_arrived(1, RIGHT_2)
    z_steps(14, 15, lambda n: eliminate_some(n + 6))
    core_arrived(1)
    z_steps(15, 18, rows_cleaned)
    z_step(jnp.int32(18))
    z_sent(0)
    z_sent(1)
    g_sent(0)
    z_step(jnp.int32(19))
    z_sent(2)
    z_sent(3)
    g_sent(1)
    z_step(jnp.int32(20))
    z_sent(4)
    z_steps(21, 24, finish)
    for hop in range(5, 8):
        z_sent(hop)


def per_device(array_volts, reference_volts):
    volts = array_volts.reshape(SUBS, PAIR, SAMPLES)
    refs = reference_volts.reshape(SUBS, 2 * NREF, SAMPLES // COLS)
    vmem = pl.BlockSpec(memory_space=pltpu.VMEM)
    hbm = pl.BlockSpec(memory_space=pltpu.HBM)
    volts = pltpu.with_memory_space_constraint(volts, pltpu.HBM)
    refs = pltpu.with_memory_space_constraint(refs, pltpu.HBM)
    return pl.pallas_call(
        kernel,
        out_shape=jax.ShapeDtypeStruct((SUBS, 2, COLS * ANTS, ROWS * ANTS), F32),
        in_specs=[hbm, hbm],
        out_specs=vmem,
        scratch_shapes=[
            pltpu.VMEM((SUBS, ROWS, PAIR, SAMPLES), BF16),
            pltpu.VMEM((SUBS, COLS, PAIR, SAMPLES), BF16),
            pltpu.VMEM((COLS, SUBS, 2 * NREF, SAMPLES // COLS), BF16),
            pltpu.VMEM((SUBS, 2 * NREF, SAMPLES), BF16),
            pltpu.VMEM((SUBS, 2, 6 * NREF, SAMPLES), BF16),
            pltpu.VMEM((SUBS, 2 * COLS * ANTS, SAMPLES), BF16),
            pltpu.VMEM((SUBS, 2 * COLS * ANTS, SAMPLES), BF16),
            pltpu.VMEM((2, SUBS, NREF, NREF), F32),
            pltpu.SemaphoreType.DMA((2, 9, SUBS)),
            pltpu.SemaphoreType.DMA((2, 9, SUBS)),
            pltpu.SemaphoreType.DMA((2, 7)),
            pltpu.SemaphoreType.DMA((2, 7)),
            pltpu.SemaphoreType.DMA((2, 8)),
            pltpu.SemaphoreType.DMA((2, 8)),
            pltpu.SemaphoreType.DMA((3,)),
        ],
        compiler_params=pltpu.CompilerParams(
            collective_id=0, has_side_effects=True, vmem_limit_bytes=48 * 1024 * 1024
        ),
    )(volts, refs)


def solution(mesh):
    return jax.shard_map(
        per_device,
        mesh=mesh,
        in_specs=(P("chan", None, ("row", "col"), None), P("chan", None, None, "col")),
        out_specs=P("chan", None, "row", "col"),
        check_vma=False,
    )
```

```python
import functools

import jax
import jax.numpy as jnp
from jax import lax
from jax.experimental import pallas as pl
from jax.experimental.pallas import tpu as pltpu
from jax.sharding import PartitionSpec as P

MESH = pl.DeviceIdType.MESH
F32, BF16 = jnp.float32, jnp.bfloat16
SUBS, NREF, ANTS, SAMPLES = 3, 32, 8, 2048
ROWS, COLS, NX = 16, 16, 4
PAIR = 2 * ANTS
LANES = 512

FROM_Y, LEFT, RIGHT, LEFT_Y, RIGHT_Y, LEFT_2, RIGHT_2, OWN = range(8)


def kernel(volts, refs, out, colb, rowb, refb, ref_all, ref_mix, hi, lo, inv, w_now, *sems):
    z_send, z_recv, g_send, g_recv, c_send, c_recv, own_sem = sems
    row, col = lax.axis_index("row"), lax.axis_index("col")
    up, down = lax.rem(row + 1, ROWS), lax.rem(row + ROWS - 1, ROWS)
    y, x, core = col // (2 * NX), lax.rem(col // 2, NX), lax.rem(col, 2)

    def at(dy, dx, other=False):
        yy = 1 - y if dy else y
        cc = 1 - core if other else core
        return yy * (2 * NX) + lax.rem(x + dx + NX, NX) * 2 + cc

    origin = {
        FROM_Y: at(1, 0), LEFT: at(0, -1), RIGHT: at(0, 1), LEFT_Y: at(1, -1),
        RIGHT_Y: at(1, 1), LEFT_2: at(0, 2), RIGHT_2: at(1, 2), OWN: col,
    }
    to_y, to_left, to_right, to_core = at(1, 0), at(0, -1), at(0, 1), at(0, 0, True)

    barrier = pltpu.get_barrier_semaphore()
    for axis, there in (
        ("row", up), ("row", down), ("col", to_y), ("col", to_left), ("col", to_right), ("col", to_core),
    ):
        pl.semaphore_signal(barrier, inc=1, device_id={axis: there}, device_id_type=MESH)
    pl.semaphore_wait(barrier, 6)

    def reach(way, start, sub):
        up_hops = 7 + jnp.asarray(sub != 1).astype(jnp.int32)
        up_hops = jnp.where(start == 8, 7, up_hops)
        up_hops = jnp.where(start == 9, 7, up_hops)
        up_hops = jnp.where(start == 10, 7, up_hops)
        up_hops = jnp.where(start == 11, 7, up_hops)
        return up_hops if way == 0 else ROWS - 1 - up_hops

    def z_start(way, hop, sub):
        return lax.rem(row + (ROWS - hop if way == 0 else hop), ROWS)

    def z_copy(way, hop, sub, mine=False):
        place = colb.at[sub, z_start(way, hop, sub)]
        return pltpu.make_async_remote_copy(
            src_ref=volts.at[sub] if mine else place,
            dst_ref=place,
            send_sem=z_send.at[way, hop, sub],
            recv_sem=z_recv.at[way, hop, sub],
            device_id={"row": up if way == 0 else down},
            device_id_type=MESH,
        )

    def z_event(way, n):
        hop, sub = n // SUBS, lax.rem(n, SUBS)
        hops = reach(way, z_start(way, hop + 1, sub), sub)

        @pl.when(hop + 1 <= hops)
        def _():
            z_copy(way, hop, sub).wait_recv()

        @pl.when(hop + 2 <= hops)
        def _():
            z_copy(way, hop + 1, sub).start()

    def z_step(n):
        z_event(0, n)
        z_event(1, n)

    def z_steps(first, last, job):
        def body(n, carry):
            z_step(n)
            job(n - first)
            return carry

        lax.fori_loop(first, last, body, jnp.int32(0))

    def z_sent(hop):
        for sub in range(SUBS):
            for way in range(2):
                if hop == 0:
                    z_copy(way, hop, sub, True).wait_send()
                else:
                    @pl.when(hop + 1 <= reach(way, z_start(way, hop, sub), sub))
                    def _():
                        z_copy(way, hop, sub).wait_send()

    def shard(kind, slot):
        return refb.at[slot] if kind == 0 else rowb.at[:, slot]

    def g_copy(kind, received, slot, there):
        mine = refs if kind == 0 else volts
        return pltpu.make_async_remote_copy(
            src_ref=mine if received in (FROM_Y, LEFT, RIGHT) else shard(kind, slot),
            dst_ref=shard(kind, slot),
            send_sem=g_send.at[kind, received],
            recv_sem=g_recv.at[kind, received],
            device_id={"col": there},
            device_id_type=MESH,
        )

    def g_send_copy(kind, received):
        slot, there = {
            FROM_Y: (col, to_y), LEFT: (col, to_right), RIGHT: (col, to_left),
            LEFT_Y: (origin[FROM_Y], to_right), RIGHT_Y: (origin[FROM_Y], to_left),
            LEFT_2: (origin[LEFT], to_right), RIGHT_2: (origin[RIGHT_Y], to_left),
        }[received]
        return g_copy(kind, received, slot, there)

    def core_copy(kind, received):
        slot = origin[received]
        mine = refs if kind == 0 else volts
        return pltpu.make_async_remote_copy(
            src_ref=mine if received == OWN else shard(kind, slot),
            dst_ref=shard(kind, slot),
            send_sem=c_send.at[kind, received],
            recv_sem=c_recv.at[kind, received],
            device_id={"col": to_core},
            device_id_type=MESH,
        )

    def g_start(kind):
        for received in (FROM_Y, LEFT, RIGHT):
            g_send_copy(kind, received).start()
        core_copy(kind, OWN).start()

    def g_arrived(kind, *those):
        for received in those:
            g_copy(kind, received, origin[received], to_left).wait_recv()
            core_copy(kind, received).start()

    def g_forward(kind, *those):
        for received in those:
            g_send_copy(kind, received).start()

    def core_arrived(kind):
        for received in range(8):
            core_copy(kind, received).wait_recv()

    def g_sent(kind):
        for received in range(7):
            g_send_copy(kind, received).wait_send()
        for received in range(8):
            core_copy(kind, received).wait_send()

    def gather_references():
        for sub in range(SUBS):
            whole = jnp.concatenate([refb[c, sub] for c in range(COLS)], axis=1)
            ref_all[sub] = whole
            real, imag = whole[:NREF], whole[NREF:]
            one = jnp.concatenate([real, -imag], axis=0)
            two = jnp.concatenate([imag, real], axis=0)
            ref_mix[sub, 0] = jnp.concatenate([one, one, one], axis=0)
            ref_mix[sub, 1] = jnp.concatenate([two, two, two], axis=0)

    def product(a, b):
        return lax.dot_general(a, b, (((1,), (1,)), ((), ())), preferred_element_type=F32)

    def covariance():
        for sub in range(SUBS):
            g = product(ref_all[sub], ref_all[sub])
            inv[0, sub] = g[:NREF, :NREF] + g[NREF:, NREF:]
            inv[1, sub] = g[NREF:, :NREF] - g[:NREF, NREF:]

    def eliminate(first, last):
        lane = lax.broadcasted_iota(jnp.int32, (SUBS, NREF, NREF), 2)
        line = lax.broadcasted_iota(jnp.int32, (SUBS, NREF, NREF), 1)

        def step(k, carry):
            re, im = carry
            on_lane, on_line = lane == k, line == k
            col_re = jnp.sum(jnp.where(on_lane, re, 0.0), axis=2, keepdims=True)
            col_im = jnp.sum(jnp.where(on_lane, im, 0.0), axis=2, keepdims=True)
            row_re = jnp.sum(jnp.where(on_line, re, 0.0), axis=1, keepdims=True)
            row_im = jnp.sum(jnp.where(on_line, im, 0.0), axis=1, keepdims=True)
            first_lane = lax.broadcasted_iota(jnp.int32, (SUBS, 1, NREF), 2) == k
            pivot = jnp.sum(jnp.where(first_lane, row_re, 0.0), axis=2, keepdims=True)
            scale = 1.0 / pivot
            row_re = jnp.where(first_lane, 1.0, row_re) * scale
            row_im = jnp.where(first_lane, 0.0, row_im) * scale
            new_re = jnp.where(on_lane, 0.0, re) - (col_re * row_re - col_im * row_im)
            new_im = jnp.where(on_lane, 0.0, im) - (col_re * row_im + col_im * row_re)
            return jnp.where(on_line, row_re, new_re), jnp.where(on_line, row_im, new_im)

        re, im = lax.fori_loop(first, last, step, (inv[0], inv[1]))
        inv[0] = re
        inv[1] = im

    def weights(sub):
        q = product(rowb[sub].reshape(COLS * PAIR, SAMPLES), ref_all[sub])
        q = q.reshape(COLS, 2, ANTS, 2 * NREF)
        cross_re = (q[:, 0, :, :NREF] + q[:, 1, :, NREF:]).reshape(COLS * ANTS, NREF)
        cross_im = (q[:, 1, :, :NREF] - q[:, 0, :, NREF:]).reshape(COLS * ANTS, NREF)
        re, im = inv[0, sub], inv[1, sub]
        cross = jnp.concatenate([cross_re, cross_im], axis=1)
        system = jnp.concatenate(
            [jnp.concatenate([re, im], axis=1), jnp.concatenate([-im, re], axis=1)], axis=0
        )
        w = jnp.dot(cross, system, precision=lax.Precision.HIGHEST, preferred_element_type=F32)
        w1 = w.astype(BF16)
        rest = w - w1.astype(F32)
        w2 = rest.astype(BF16)
        w3 = (rest - w2.astype(F32)).astype(BF16)
        return jnp.concatenate([w1, w2, w3], axis=1)

    def clean_rows(sub, w, part):
        here = pl.ds(part * LANES, LANES)
        raw = rowb[sub, :, :, here].astype(F32).reshape(COLS, 2, ANTS, LANES)
        for p in range(2):
            one = raw[:, p].reshape(COLS * ANTS, LANES)
            one = one - jnp.dot(w, ref_mix[sub, p, :, here], preferred_element_type=F32)
            top = one.astype(BF16)
            hi[sub, pl.ds(p * 128, 128), here] = top
            lo[sub, pl.ds(p * 128, 128), here] = (one - top.astype(F32)).astype(BF16)

    def finish(sub):
        b = colb[sub].reshape(ROWS * PAIR, SAMPLES)
        t = product(b, hi[sub]) + product(b, lo[sub])
        t = t.reshape(ROWS, 2, ANTS, 256)
        re = (t[:, 0, :, :128] + t[:, 1, :, 128:]).reshape(ROWS * ANTS, 128)
        im = (t[:, 0, :, 128:] - t[:, 1, :, :128]).reshape(ROWS * ANTS, 128)
        out[sub, 0] = re.T * (1.0 / SAMPLES)
        out[sub, 1] = im.T * (1.0 / SAMPLES)

    for sub in range(SUBS):
        for way in range(2):
            z_copy(way, 0, sub, True).start()
        if sub == 0:
            g_start(0)
    g_start(1)
    own = [
        pltpu.make_async_copy(volts, colb.at[:, row], own_sem.at[0]),
        pltpu.make_async_copy(volts, rowb.at[:, col], own_sem.at[1]),
        pltpu.make_async_copy(refs, refb.at[col], own_sem.at[2]),
    ]
    for copy in own:
        copy.start()

    def rows_first():
        g_arrived(1, FROM_Y, LEFT, RIGHT)
        g_forward(1, LEFT_Y, RIGHT_Y, LEFT_2)

    def rows_second():
        g_arrived(1, LEFT_Y, RIGHT_Y)
        g_forward(1, RIGHT_2)

    def refs_first():
        g_arrived(0, FROM_Y, LEFT, RIGHT)
        g_forward(0, LEFT_Y, RIGHT_Y, LEFT_2)

    def refs_second():
        g_arrived(0, LEFT_Y, RIGHT_Y, LEFT_2)
        g_forward(0, RIGHT_2)

    def refs_here():
        core_arrived(0)
        gather_references()

    def eliminate_some(n):
        eliminate(5 * n, jnp.minimum(5 * n + 5, NREF))

    after = {
        1: [refs_first], 3: [refs_second], 4: [rows_first], 5: [functools.partial(g_arrived, 0, RIGHT_2)],
        6: [refs_here], 7: [covariance],
    }
    for n in range(8):
        z_step(jnp.int32(n))
        if n == 2:
            for copy in own:
                copy.wait()
        for job in after.get(n, ()):
            job()
    z_steps(8, 9, eliminate_some)
    g_arrived(1, RIGHT_Y)
    g_forward(1, RIGHT_2)
    z_steps(9, 12, lambda n: eliminate_some(n + 1))
    g_arrived(1, LEFT_Y, LEFT_2)
    z_steps(12, 14, lambda n: eliminate_some(n + 4))
    g_arrived(1, RIGHT_2)
    z_steps(14, 15, lambda n: eliminate_some(n + 6))
    core_arrived(1)
    def rows_part(n):
        sub = n // 2

        @pl.when(lax.rem(n, 2) == 0)
        def _():
            w_now[...] = weights(sub)

        @pl.when(lax.rem(n, 2) == 1)
        def _():
            for part in range(SAMPLES // LANES):
                clean_rows(sub, w_now[...], part)

    z_steps(15, 21, rows_part)
    for hop in range(5):
        z_sent(hop)
    g_sent(0)
    g_sent(1)
    z_steps(21, 24, finish)
    for hop in range(5, 8):
        z_sent(hop)


def per_device(array_volts, reference_volts):
    volts = array_volts.reshape(SUBS, PAIR, SAMPLES)
    refs = reference_volts.reshape(SUBS, 2 * NREF, SAMPLES // COLS)
    vmem = pl.BlockSpec(memory_space=pltpu.VMEM)
    hbm = pl.BlockSpec(memory_space=pltpu.HBM)
    volts = pltpu.with_memory_space_constraint(volts, pltpu.HBM)
    refs = pltpu.with_memory_space_constraint(refs, pltpu.HBM)
    return pl.pallas_call(
        kernel,
        out_shape=jax.ShapeDtypeStruct((SUBS, 2, COLS * ANTS, ROWS * ANTS), F32),
        in_specs=[hbm, hbm],
        out_specs=vmem,
        scratch_shapes=[
            pltpu.VMEM((SUBS, ROWS, PAIR, SAMPLES), BF16),
            pltpu.VMEM((SUBS, COLS, PAIR, SAMPLES), BF16),
            pltpu.VMEM((COLS, SUBS, 2 * NREF, SAMPLES // COLS), BF16),
            pltpu.VMEM((SUBS, 2 * NREF, SAMPLES), BF16),
            pltpu.VMEM((SUBS, 2, 6 * NREF, SAMPLES), BF16),
            pltpu.VMEM((SUBS, 2 * COLS * ANTS, SAMPLES), BF16),
            pltpu.VMEM((SUBS, 2 * COLS * ANTS, SAMPLES), BF16),
            pltpu.VMEM((2, SUBS, NREF, NREF), F32),
            pltpu.VMEM((COLS * ANTS, 6 * NREF), BF16),
            pltpu.SemaphoreType.DMA((2, 9, SUBS)),
            pltpu.SemaphoreType.DMA((2, 9, SUBS)),
            pltpu.SemaphoreType.DMA((2, 7)),
            pltpu.SemaphoreType.DMA((2, 7)),
            pltpu.SemaphoreType.DMA((2, 8)),
            pltpu.SemaphoreType.DMA((2, 8)),
            pltpu.SemaphoreType.DMA((3,)),
        ],
        compiler_params=pltpu.CompilerParams(
            collective_id=0, has_side_effects=True, vmem_limit_bytes=48 * 1024 * 1024
        ),
    )(volts, refs)


def solution(mesh):
    return jax.shard_map(
        per_device,
        mesh=mesh,
        in_specs=(P("chan", None, ("row", "col"), None), P("chan", None, None, "col")),
        out_specs=P("chan", None, "row", "col"),
        check_vma=False,
    )
```
